512 devices in a mesh: turn: 128 (over x_hi, z, y), tm: 4 (over x_lo, core).
Axes of the slice: x: 4 (x_hi: 2, x_lo: 2; x = x_hi * 2 + x_lo), y: 4, z: 16, core: 2. Of those that a mesh axis runs over, the one named last changes fastest.
Arguments:
- voltages: bfloat16 [2048, 32768], P('turn', 'tm'), may hold values from -6 to 6
- gains: float32 [2, 2048, 1024], P(None, None, 'turn'), may hold values from -5 to 5
- dispersion: float32 [1024], P('turn'), may hold values from 50 to 400
Outputs:
- wideband: float32 [1024, 2, 32768], P('turn', None, 'tm')
The draws below stay inside these ranges and needn't reach their ends.
All inputs are finite; a program needn't handle non-finite values.
Results may differ from the reference program's by a relative error of at most 0.0079.
Values may be sent and summed in bfloat16 or wider, within the bound.
A program may use at most 64 MiB of HBM per device.

```python
import math
import jax
import jax.numpy as jnp
from jax import lax

CHANNELS = 1024
NFFT = 2048
TAPS = 4
POLS = 2
CYL = 4
FEEDS = 256
INPUTS = 2048
BEAMS = 1024
FRAMES = 16
SAMPLES = 32768


def levels(stream_key, shape, split, smallest, top_value):
    level, own = 1.0, jax.random.fold_in(stream_key, 6)
    for axis_at, blocks in split:
        steps = jnp.exp(jax.random.uniform(jax.random.fold_in(own, axis_at), (blocks,), jnp.float32, smallest / len(split), top_value / len(split)))
        level = level * jnp.repeat(steps, shape[axis_at] // blocks).reshape([-1 if axis == axis_at else 1 for axis in range(len(shape))])
    return level


def noise(rng, shape, scale, bound, shards=(), kind=jnp.bfloat16):
    drawn = jax.random.normal(rng, shape, jnp.float32) * scale
    if len(shards) > 0:
        drawn = levels(rng, shape, shards, -0.22, 0.18) * drawn
    return jnp.clip(drawn, min=-bound, max=bound).astype(kind)


def setup_inputs(seed: int = 0) -> dict:
    streams_of = jax.random.split(jax.random.key(seed), 4)
    return {
        "voltages": noise(streams_of[0], (INPUTS, SAMPLES), 1.0, 6.0, ((0, 128), (1, 4))),
        "gains": noise(streams_of[1], (2, INPUTS, CHANNELS), 1.0, 5.0, ((2, 128),), jnp.float32),
        "dispersion": jnp.clip(jnp.exp(math.log(400.0) - 2.0794415 * jax.random.uniform(streams_of[2], (BEAMS,), jnp.float32) ** levels(streams_of[2], (BEAMS,), ((0, 128),), -0.2, 0.2)), 50.0, 400.0),
    }


def dft_table(length):
    half_len = length // 2
    sample_idx = jnp.arange(length, dtype=jnp.int32)
    channel_idx = jnp.arange(half_len, dtype=jnp.int32)
    product = sample_idx[:, None] * channel_idx[None, :] % length
    radians = product.astype(jnp.float32) * (2.0 * math.pi / length)
    return jnp.concatenate([jnp.cos(radians).astype(jnp.bfloat16), (-jnp.sin(radians)).astype(jnp.bfloat16)], axis=1)

def feed_table(length):
    feed_idx = jnp.arange(length, dtype=jnp.int32)
    product = feed_idx[:, None] * feed_idx[None, :] % length
    radians = product.astype(jnp.float32) * (2.0 * math.pi / length)
    cosine = jnp.cos(radians)
    sine_part = jnp.sin(radians)
    upper = jnp.concatenate([cosine, -sine_part], axis=1)
    lower = jnp.concatenate([sine_part, cosine], axis=1)
    return jnp.concatenate([upper, lower], axis=0).astype(jnp.bfloat16)

def window_table():
    extent = TAPS * NFFT
    centres = jnp.arange(extent, dtype=jnp.int32).astype(jnp.float32) + 0.5
    shape_fn = jnp.sinc((centres - 0.5 * extent) / NFFT) * (0.5 - 0.5 * jnp.cos(centres * (2.0 * math.pi / extent)))
    return shape_fn.reshape(TAPS, NFFT)

def quarter_tables():
    cyl_idx = jnp.arange(CYL, dtype=jnp.int32)
    quarter = cyl_idx[:, None] * cyl_idx[None, :] % 4
    cosine = jnp.where(quarter == 0, 1.0, jnp.where(quarter == 2, -1.0, 0.0)).astype(jnp.float32)
    sine_part = jnp.where(quarter == 1, 1.0, jnp.where(quarter == 3, -1.0, 0.0)).astype(jnp.float32)
    return (cosine, sine_part)

def frame_sums(extended, window, number):
    running = window[0] * extended[:, 0:number]
    for tap_idx in range(1, TAPS):
        running = running + window[tap_idx] * extended[:, tap_idx:tap_idx + number]
    return running

def synth_sums(extended, window, number):
    running = window[TAPS - 1] * extended[:, :, :, 0:number]
    for tap_idx in range(1, TAPS):
        running = running + window[TAPS - 1 - tap_idx] * extended[:, :, :, tap_idx:tap_idx + number]
    return running

def beam_feeds(turned, gains, feed_mat):
    number = turned.shape[1]
    channels_here = turned.shape[3]
    real_in = turned[:, :, 0].astype(jnp.float32)
    imag_in = turned[:, :, 1].astype(jnp.float32)
    gain_re = gains[0][:, None, :]
    gain_im = gains[1][:, None, :]
    calibrated = jnp.stack([gain_re * real_in - gain_im * imag_in, gain_re * imag_in + gain_im * real_in], axis=2).astype(jnp.bfloat16)
    calibrated = calibrated.reshape(POLS, CYL, FEEDS, number, 2, channels_here).transpose(5, 3, 0, 1, 4, 2)
    spread = jnp.dot(calibrated.reshape(-1, 2 * FEEDS), feed_mat, preferred_element_type=jnp.float32) * (1.0 / math.sqrt(FEEDS))
    return spread.reshape(channels_here, number, POLS, CYL, 2, FEEDS).astype(jnp.bfloat16)

def widened(values):
    return lax.optimization_barrier(values).astype(jnp.float32)

def east_west(spread):
    cosine, sine_part = quarter_tables()
    highest = lax.Precision.HIGHEST
    real_in = spread[:, :, :, :, 0]
    imag_in = spread[:, :, :, :, 1]
    real_out = jnp.einsum('ec,tfpcn->tfpen', cosine, real_in, precision=highest) + jnp.einsum('ec,tfpcn->tfpen', sine_part, imag_in, precision=highest)
    imag_out = jnp.einsum('ec,tfpcn->tfpen', cosine, imag_in, precision=highest) - jnp.einsum('ec,tfpcn->tfpen', sine_part, real_in, precision=highest)
    return 0.5 * jnp.stack([real_out, imag_out], axis=4)

def synthesise(beams_in, dispersion, table):
    channels_here = beams_in.shape[0]
    number = beams_in.shape[1]
    beams_here = beams_in.shape[5]
    ordered = beams_in.transpose(5, 3, 2, 1, 4, 0)
    freq_idx = jnp.arange(channels_here, dtype=jnp.int32).astype(jnp.float32)
    spacing = 1.0 / (1.0 + freq_idx / channels_here) ** 2
    radians = dispersion.reshape(beams_here, CYL)[:, :, None] * spacing[None, None, :]
    cosine = jnp.cos(radians)[:, :, None, None, :]
    sine_part = jnp.sin(radians)[:, :, None, None, :]
    real_in = ordered[:, :, :, :, 0]
    imag_in = ordered[:, :, :, :, 1]
    chirped = jnp.stack([real_in * cosine - imag_in * sine_part, real_in * sine_part + imag_in * cosine], axis=4).astype(jnp.bfloat16)
    waveform = lax.dot_general(chirped.reshape(-1, 2 * channels_here), table, (((1,), (1,)), ((), ())), preferred_element_type=jnp.float32) * (1.0 / math.sqrt(NFFT))
    return waveform.astype(jnp.bfloat16).reshape(beams_here, CYL, POLS, number, NFFT)

def reference(voltages, gains, dispersion):
    table = dft_table(NFFT)
    window = window_table()
    feed_mat = feed_table(FEEDS)
    samples_in = voltages.reshape(INPUTS, FRAMES, NFFT).astype(jnp.float32)
    extended = jnp.concatenate([jnp.zeros((INPUTS, TAPS - 1, NFFT), jnp.float32), samples_in], axis=1)
    summed = frame_sums(extended, window, FRAMES).astype(jnp.bfloat16)
    channel = (jnp.dot(summed.reshape(-1, NFFT), table, preferred_element_type=jnp.float32) * (1.0 / math.sqrt(NFFT))).astype(jnp.bfloat16)
    channel = channel.reshape(INPUTS, FRAMES, 2, CHANNELS)
    spread = beam_feeds(channel, gains, feed_mat)
    waves_out = synthesise(east_west(widened(spread)), dispersion, table)
    padded = jnp.concatenate([waves_out, jnp.zeros((FEEDS, CYL, POLS, TAPS - 1, NFFT), jnp.bfloat16)], axis=3).astype(jnp.float32)
    result = synth_sums(padded, window, FRAMES)
    return result.reshape(BEAMS, POLS, SAMPLES)
```

```python
import functools
import math

import jax
import jax.numpy as jnp
import ml_dtypes
import numpy as np
from jax import lax
from jax.experimental import pallas as pl
from jax.experimental.pallas import tpu as pltpu
from jax.sharding import PartitionSpec as P

NFFT = 2048
TAPS = 4
FRAMES = 4
GROUP = 16
QUADS = 8
FEEDS = 256
SHORT = 256
BF16 = jnp.bfloat16
F32 = jnp.float32
MESH = pl.DeviceIdType.MESH
HALF_ROOT = math.sqrt(0.5)


def window_rows():
    extent = TAPS * NFFT
    t = np.arange(extent, dtype=np.float64) + 0.5
    shape = np.sinc((t - 0.5 * extent) / NFFT) * (0.5 - 0.5 * np.cos(t * (2.0 * np.pi / extent)))
    return shape.reshape(TAPS, NFFT).astype(np.float32)


def twiddle_rows():
    angle = 2.0 * np.pi * np.outer(np.arange(8), np.arange(SHORT)) / NFFT
    return (np.stack([np.cos(angle), np.sin(angle)], axis=1) / math.sqrt(NFFT)).astype(np.float32)


def forward_table():
    g, q = np.meshgrid(np.arange(GROUP), np.arange(QUADS), indexing="ij")
    k2 = 16 * q + g
    angle = 2.0 * np.pi * (k2[:, :, None] * np.arange(SHORT) % SHORT) / SHORT
    c, s = np.cos(angle), np.sin(angle)
    real = np.concatenate([c, s], axis=-1)
    imag = np.concatenate([-s, c], axis=-1)
    return np.stack([real, imag], axis=1).reshape(256, 512).astype(ml_dtypes.bfloat16)


def inverse_table():
    g, q = np.meshgrid(np.arange(GROUP), np.arange(QUADS), indexing="ij")
    k2 = (16 * q + g).reshape(-1)
    angle = 2.0 * np.pi * (np.outer(k2, np.arange(SHORT)) % SHORT) / SHORT
    c, s = np.cos(angle), np.sin(angle)
    real = np.concatenate([c, s], axis=1)
    imag = np.concatenate([-s, c], axis=1)
    return np.concatenate([real, imag], axis=0).astype(ml_dtypes.bfloat16)


def beam_table():
    feed = np.arange(FEEDS)
    angle = 2.0 * np.pi * (np.outer(feed, feed) % FEEDS) / FEEDS
    c = np.cos(angle).astype(np.float32).astype(ml_dtypes.bfloat16).astype(np.float32)
    s = np.sin(angle).astype(np.float32).astype(ml_dtypes.bfloat16).astype(np.float32)
    real = np.concatenate([c.T, s.T], axis=1)
    imag = np.concatenate([-s.T, c.T], axis=1)
    both = np.stack([real, imag], axis=1).reshape(32, 4, 2, 2, 512).transpose(1, 0, 2, 3, 4)
    return (both.reshape(512, 512) / 16.0).astype(ml_dtypes.bfloat16)


def spacing_rows():
    g = np.arange(GROUP)[:, None, None, None]
    k1 = np.arange(8)[None, None, :, None]
    q = np.arange(QUADS)[None, None, None, :]
    k = (128 * q + 8 * g + k1 + np.zeros((1, 2, 1, 1), np.int64)).astype(np.float32)
    base = np.float32(1.0) + k / np.float32(1024.0)
    return (np.float32(1.0) / (base * base)).reshape(GROUP, 128).astype(np.float32)


def swap(low, high, axis, by):
    rank = low.ndim
    index = lax.broadcasted_iota(jnp.int32, low.shape, rank - 2 + axis)
    first = (index & by) == 0
    size = low.shape[rank - 2 + axis]
    if axis == 1:
        flat = (-1, low.shape[-1])
        up = pltpu.roll(high.reshape(flat), by, 1).reshape(low.shape)
        down = pltpu.roll(low.reshape(flat), size - by, 1).reshape(low.shape)
    else:
        up = pltpu.roll(high, by, rank - 2)
        down = pltpu.roll(low, size - by, rank - 2)
    return jnp.where(first, low, up), jnp.where(first, down, high)


def exchange(x, bits, lane):
    shape = x.shape
    for b in range(bits):
        split = x.reshape((2 ** (bits - 1 - b), 2, 2**b) + shape[1:])
        low, high = swap(split[:, 0], split[:, 1], 1, lane << b)
        x = jnp.stack([low, high], axis=1).reshape(shape)
    return x


def eight_forward(x):
    s04, d04, s26, d26 = x[0] + x[4], x[0] - x[4], x[2] + x[6], x[2] - x[6]
    s15, d15, s37, d37 = x[1] + x[5], x[1] - x[5], x[3] + x[7], x[3] - x[7]
    even, odd = s04 + s26, s15 + s37
    near, far = HALF_ROOT * (d15 - d37), HALF_ROOT * (d15 + d37)
    y1 = (d04 + near, -(d26 + far))
    y2 = (s04 - s26, s37 - s15)
    y3 = (d04 - near, d26 - far)
    return (even + odd, None), y1, y2, y3, (even - odd, None)


def eight_inverse(a0, a1, a2, a3, a4, b1, b2, b3):
    plus, minus = a0 + a4, a0 - a4
    a13, a31 = a1 + a3, HALF_ROOT * (a1 - a3)
    b13, b31 = HALF_ROOT * (b1 + b3), b1 - b3
    o0, o2 = plus + a2, plus - a2
    m1, m3 = minus - b2, minus + b2
    return (
        o0 + a13, m1 + a31 - b13, o2 - b31, m3 - a31 - b13,
        o0 - a13, m1 - a31 + b13, o2 + b31, m3 + a31 + b13,
    )


def turned_phase(turns):
    return jnp.cos(turns), jnp.sin(turns)


def kernel(
    volt, gain, disp, window, twid, fwd, inv, beam, space, out,
    xv, xh, gv, wv, tv, fv, iv, bv, sv, gb, gr, gt, zs, ab, ra, xs, sb, sr, ct, vs, ys, wf, wb, wr, ov,
    load_sem, out_sem, send_sem, recv_sem,
):
    me, tm = lax.axis_index("turn"), lax.axis_index("tm")
    base, g = (me // GROUP) * GROUP, me % GROUP
    xz, y = me // 4, me % 4
    after, before = (tm + 1) % 4, (tm + 3) % 4

    barrier = pltpu.get_barrier_semaphore()

    def greet_group(i, _):
        pl.semaphore_signal(barrier, inc=1, device_id={"turn": base + (g + i) % GROUP}, device_id_type=MESH)
        return 0

    def greet_quads(i, _):
        pl.semaphore_signal(barrier, inc=1, device_id={"turn": (me + GROUP * i) % 128}, device_id_type=MESH)
        return 0

    for other in (after, before):
        pl.semaphore_signal(barrier, inc=1, device_id={"tm": other}, device_id_type=MESH)
    lax.fori_loop(1, QUADS, greet_quads, 0)
    lax.fori_loop(1, GROUP, greet_group, 0)

    loads = [
        pltpu.make_async_copy(a, b, load_sem.at[i])
        for i, (a, b) in enumerate(
            [(volt, xv), (gain, gv), (window, wv), (twid, tv), (fwd, fv), (inv, iv), (beam, bv), (space, sv)]
        )
    ]
    for load in loads:
        load.start()
    loads[0].wait()
    loads[1].wait()
    gb[...] = gv[...].reshape(16, 2048).astype(BF16)
    pl.semaphore_wait(barrier, 2 + QUADS - 1 + GROUP - 1)

    history = pltpu.make_async_remote_copy(
        src_ref=xv.at[:, pl.ds(NFFT, 3 * NFFT)], dst_ref=xh, send_sem=send_sem.at[0], recv_sem=recv_sem.at[0],
        device_id={"tm": after}, device_id_type=MESH,
    )
    history.start()

    mine = me // GROUP

    def send_gain(i, _):
        q = (mine + i) % QUADS
        pltpu.make_async_remote_copy(
            src_ref=gb.at[:, pl.ds(pl.multiple_of(q * FEEDS, FEEDS), FEEDS)], dst_ref=gr.at[mine],
            send_sem=send_sem.at[1], recv_sem=recv_sem.at[1],
            device_id={"turn": q * GROUP + g}, device_id_type=MESH,
        ).start()
        return 0

    lax.fori_loop(1, QUADS, send_gain, 0)
    gr[mine] = gb[:, pl.ds(pl.multiple_of(mine * FEEDS, FEEDS), FEEDS)]

    for i in (2, 3, 4):
        loads[i].wait()
    keep = jnp.where(tm > 0, 1.0, 0.0).astype(F32)

    def frame_of(at):
        if at < 0:
            return xh[:, pl.ds((at + 3) * NFFT, NFFT)].astype(F32) * keep
        return xv[:, pl.ds(at * NFFT, NFFT)].astype(F32)

    def channelize(f):
        total = wv[0:1, :] * frame_of(f - 3)
        for p in range(1, TAPS):
            total = total + wv[p : p + 1, :] * frame_of(f - 3 + p)
        total = total.astype(BF16).astype(F32)
        parts = eight_forward([total[:, n * SHORT : (n + 1) * SHORT] for n in range(8)])
        for k1 in range(8):
            re, im = parts[k1] if k1 < 5 else parts[8 - k1]
            c, s = tv[k1, 0:1, :], -tv[k1, 1:2, :]
            if im is None:
                zr, zi = re * c, re * s
            elif k1 < 5:
                zr, zi = re * c - im * s, re * s + im * c
            else:
                zr, zi = re * c + im * s, re * s - im * c
            rows = pl.ds((f * 8 + k1) * 16, 16)
            zs[rows, 0:SHORT] = zr.astype(BF16)
            zs[rows, SHORT : 2 * SHORT] = zi.astype(BF16)

    channelize(3)
    history.wait_recv()
    for f in range(3):
        channelize(f)
    contract = (((1,), (1,)), ((), ()))
    ab[...] = lax.dot_general(fv[...], zs[...], contract, preferred_element_type=F32).astype(BF16)

    def send_channels(i, _):
        to = (g + i) % GROUP
        pltpu.make_async_remote_copy(
            src_ref=ab.at[pl.ds(pl.multiple_of(to * 16, 16), 16), :], dst_ref=ra.at[g],
            send_sem=send_sem.at[2], recv_sem=recv_sem.at[2],
            device_id={"turn": base + to}, device_id_type=MESH,
        ).start()
        return 0

    lax.fori_loop(1, GROUP, send_channels, 0)
    ra[g] = ab[pl.ds(pl.multiple_of(g * 16, 16), 16), :]

    pltpu.make_async_copy(gr.at[pl.ds(0, QUADS - 1)], gr.at[pl.ds(0, QUADS - 1)], recv_sem.at[1]).wait()
    for half in range(2):
        got = gr[:, :, half * 128 : (half + 1) * 128].astype(F32).reshape(QUADS, 2, 8, 128)
        for b in range(3):
            split = got.reshape(2 ** (2 - b), 2, 2**b, 2, 8, 128)
            flat = (-1, 8, 128)
            low, high = swap(split[:, 0].reshape(flat), split[:, 1].reshape(flat), 0, 1 << b)
            part = (2 ** (2 - b), 2**b, 2, 8, 128)
            got = jnp.stack([low.reshape(part), high.reshape(part)], axis=1).reshape(QUADS, 2, 8, 128)
        gt[half] = got

    loads[7].wait()
    row = lax.broadcasted_iota(jnp.int32, (8, 128), 0)

    def phases(at, _):
        for e in range(4):
            scale = jnp.where((row & 2) == 0, disp[e], disp[4 + e])
            c, s = turned_phase(scale * sv[pl.ds(at, 1), :])
            ct[at, 0, e] = 0.5 * c
            ct[at, 1, e] = 0.5 * s
        return 0

    lax.fori_loop(0, GROUP, phases, 0)

    loads[6].wait()
    loads[5].wait()
    pltpu.make_async_copy(ra.at[pl.ds(0, GROUP - 1)], ra.at[pl.ds(0, GROUP - 1)], recv_sem.at[2]).wait()

    for f in range(FRAMES):
        for half in range(2):
            got = ra[half * 8 : (half + 1) * 8, :, f * 128 : (f + 1) * 128].astype(F32)
            got = exchange(got.reshape(8, 2, 8, 128), 3, 16)
            re, im = got[:, 0], got[:, 1]
            gre, gim = gt[half, :, 0], gt[half, :, 1]
            rows = pl.ds(f * 64, 64)
            xs[rows, half * 128 : (half + 1) * 128] = (gre * re - gim * im).reshape(64, 128).astype(BF16)
            xs[rows, FEEDS + half * 128 : FEEDS + (half + 1) * 128] = (gre * im + gim * re).reshape(64, 128).astype(BF16)

    row3 = lax.broadcasted_iota(jnp.int32, (16, 8, 128), 1)
    for c in range(4):
        to_y = (y + c) % 4
        both = lax.dot_general(
            bv[pl.ds(pl.multiple_of(to_y * 128, 128), 128), :], xs[...], contract, preferred_element_type=F32
        )
        low, high = both[:, :128].reshape(16, 8, 128), both[:, 128:].reshape(16, 8, 128)
        sb[to_y, :, 0] = jnp.where(row3 < 4, low, pltpu.roll(high, 4, 1)).astype(BF16)
        sb[to_y, :, 1] = jnp.where(row3 < 4, pltpu.roll(low, 4, 1), high).astype(BF16)

        def send_beams(i, _):
            to = (xz + i) % 32
            pltpu.make_async_remote_copy(
                src_ref=sb.at[to_y, to // 2, to % 2], dst_ref=sr.at[me],
                send_sem=send_sem.at[3], recv_sem=recv_sem.at[3],
                device_id={"turn": to * 4 + to_y}, device_id_type=MESH,
            ).start()
            return 0

        lax.fori_loop(1 if c == 0 else 0, 32, send_beams, 0)
    sr[me] = sb[y, xz // 2, xz % 2]

    pltpu.make_async_copy(sr.at[pl.ds(0, 127)], sr.at[pl.ds(0, 127)], recv_sem.at[3]).wait()

    def east_west(at, _):
        ns = [[None] * 4, [None] * 4]
        for c in range(4):
            one = sr[c * GROUP + at].astype(F32)
            two = sr[64 + c * GROUP + at].astype(F32)
            ns[0][c], ns[1][c] = swap(one, two, 0, 1)
        (r0, r1, r2, r3), (i0, i1, i2, i3) = ns
        ra_, rb_, rc_, rd_ = r0 + r2, r0 - r2, r1 + r3, r1 - r3
        ia_, ib_, ic_, id_ = i0 + i2, i0 - i2, i1 + i3, i1 - i3
        beams = [(ra_ + rc_, ia_ + ic_), (rb_ + id_, ib_ - rd_), (ra_ - rc_, ia_ - ic_), (rb_ - id_, ib_ + rd_)]
        chirped = []
        for e in range(4):
            re, im = beams[e]
            c, s = ct[at, 0, e], ct[at, 1, e]
            chirped.append((re * c - im * s, re * s + im * c))
        for high in range(2):
            for r in range(2):
                first, second = swap(chirped[2 * high][r], chirped[2 * high + 1][r], 0, 4)
                vs[r, 0, at, high] = first
                vs[r, 1, at, high] = second
        return 0

    lax.fori_loop(0, GROUP, east_west, 0)

    for r in range(2):
        for h in range(2):
            turned = exchange(vs[r, h], 4, 8).reshape(2, 8, 16, 128).astype(BF16)
            ys[2 * h, :, :, r * 128 : (r + 1) * 128] = turned[0]
            ys[2 * h + 1, :, :, r * 128 : (r + 1) * 128] = turned[1]

    def synthesise(f):
        z = jnp.dot(ys[f].reshape(128, 256), iv[...], preferred_element_type=F32).reshape(8, 16, 512)
        re, im = [], []
        for k1 in range(8):
            zr, zi = z[k1, :, :SHORT], z[k1, :, SHORT:]
            c, s = tv[k1, 0:1, :], tv[k1, 1:2, :]
            re.append(zr * c - zi * s)
            im.append(zr * s + zi * c if k1 % 4 else None)
        outs = eight_inverse(
            re[0], re[1] + re[7], re[2] + re[6], re[3] + re[5], re[4],
            im[1] - im[7], im[2] - im[6], im[3] - im[5],
        )
        for n in range(8):
            wf[f, :, n * SHORT : (n + 1) * SHORT] = outs[n]
            if f < 3:
                wb[f, :, n * SHORT : (n + 1) * SHORT] = outs[n].astype(BF16)

    for f in range(3):
        synthesise(f)
    future = pltpu.make_async_remote_copy(
        src_ref=wb, dst_ref=wr, send_sem=send_sem.at[4], recv_sem=recv_sem.at[4],
        device_id={"tm": before}, device_id_type=MESH,
    )
    future.start()
    synthesise(3)

    last = jnp.where(tm < 3, 1.0, 0.0).astype(F32)

    def wave_of(at):
        if at > 3:
            return wr[at - 4].astype(F32) * last
        return wf[at]

    stores = []
    for f in range(FRAMES):
        if f == 1:
            future.wait_recv()
        total = wv[3:4, :] * wave_of(f)
        for p in range(1, TAPS):
            total = total + wv[3 - p : 4 - p, :] * wave_of(f + p)
        ov[:, f * NFFT : (f + 1) * NFFT] = total
        store = pltpu.make_async_copy(
            ov.at[:, pl.ds(f * NFFT, NFFT)], out.at[:, pl.ds(f * NFFT, NFFT)], out_sem.at[f]
        )
        store.start()
        stores.append(store)

    history.wait_send()
    future.wait_send()
    pltpu.make_async_copy(gr.at[pl.ds(0, QUADS - 1)], gr.at[pl.ds(0, QUADS - 1)], send_sem.at[1]).wait()
    pltpu.make_async_copy(ra.at[pl.ds(0, GROUP - 1)], ra.at[pl.ds(0, GROUP - 1)], send_sem.at[2]).wait()
    pltpu.make_async_copy(sr.at[pl.ds(0, 127)], sr.at[pl.ds(0, 127)], send_sem.at[3]).wait()
    for store in stores:
        store.wait()


def body(voltages, gains, dispersion):
    anywhere = pl.BlockSpec(memory_space=pl.ANY)
    vmem = pltpu.VMEM
    rows = pl.pallas_call(
        kernel,
        out_shape=jax.ShapeDtypeStruct((16, FRAMES * NFFT), F32),
        in_specs=[anywhere, anywhere, pl.BlockSpec(memory_space=pltpu.SMEM)] + [anywhere] * 6,
        out_specs=anywhere,
        scratch_shapes=[
            vmem((16, FRAMES * NFFT), BF16),
            vmem((16, 3 * NFFT), BF16),
            vmem((2, 8, 2048), F32),
            vmem((TAPS, NFFT), F32),
            vmem((8, 2, SHORT), F32),
            vmem((256, 512), BF16),
            vmem((256, 512), BF16),
            vmem((512, 512), BF16),
            vmem((GROUP, 128), F32),
            vmem((16, 2048), BF16),
            vmem((QUADS, 16, FEEDS), BF16),
            vmem((2, 8, 2, 8, 128), F32),
            vmem((512, 512), BF16),
            vmem((256, 512), BF16),
            vmem((GROUP, 16, 512), BF16),
            vmem((256, 512), BF16),
            vmem((4, 16, 2, 8, 128), BF16),
            vmem((128, 8, 128), BF16),
            vmem((GROUP, 2, 4, 8, 128), F32),
            vmem((2, 2, GROUP, 2, 8, 128), F32),
            vmem((FRAMES, 8, 16, 256), BF16),
            vmem((FRAMES, 16, NFFT), F32),
            vmem((3, 16, NFFT), BF16),
            vmem((3, 16, NFFT), BF16),
            vmem((16, FRAMES * NFFT), F32),
            pltpu.SemaphoreType.DMA((8,)),
            pltpu.SemaphoreType.DMA((FRAMES,)),
            pltpu.SemaphoreType.DMA((5,)),
            pltpu.SemaphoreType.DMA((5,)),
        ],
        compiler_params=pltpu.CompilerParams(
            collective_id=0, has_side_effects=True, vmem_limit_bytes=40 * 1024 * 1024
        ),
        cost_estimate=pl.CostEstimate(flops=500_000_000, bytes_accessed=3_000_000, transcendentals=0),
    )(
        voltages, gains.transpose(0, 2, 1), dispersion,
        window_rows(), twiddle_rows(), forward_table(), inverse_table(), beam_table(), spacing_rows(),
    )
    ordered = rows.reshape(4, 2, 2, FRAMES * NFFT).transpose(1, 0, 2, 3)
    return ordered.reshape(8, 2, FRAMES * NFFT)


def solution(mesh):
    placed = (P("turn", "tm"), P(None, None, "turn"), P("turn"))
    return jax.shard_map(
        body, mesh=mesh, in_specs=placed, out_specs=P("turn", None, "tm"), check_vma=False
    )
```

```python
import functools
import math

import jax
import jax.numpy as jnp
import ml_dtypes
import numpy as np
from jax import lax
from jax.experimental import pallas as pl
from jax.experimental.pallas import tpu as pltpu
from jax.sharding import PartitionSpec as P

NFFT = 2048
TAPS = 4
FRAMES = 4
GROUP = 16
QUADS = 8
FEEDS = 256
SHORT = 256
BF16 = jnp.bfloat16
F32 = jnp.float32
MESH = pl.DeviceIdType.MESH
HALF_ROOT = math.sqrt(0.5)


def window_rows():
    extent = TAPS * NFFT
    t = np.arange(extent, dtype=np.float64) + 0.5
    shape = np.sinc((t - 0.5 * extent) / NFFT) * (0.5 - 0.5 * np.cos(t * (2.0 * np.pi / extent)))
    return shape.reshape(TAPS, NFFT).astype(np.float32)


def twiddle_rows():
    angle = 2.0 * np.pi * np.outer(np.arange(8), np.arange(SHORT)) / NFFT
    return (np.stack([np.cos(angle), np.sin(angle)], axis=1) / math.sqrt(NFFT)).astype(np.float32)


def forward_table():
    g, q = np.meshgrid(np.arange(GROUP), np.arange(QUADS), indexing="ij")
    k2 = 16 * q + g
    angle = 2.0 * np.pi * (k2[:, :, None] * np.arange(SHORT) % SHORT) / SHORT
    c, s = np.cos(angle), np.sin(angle)
    real = np.concatenate([c, s], axis=-1)
    imag = np.concatenate([-s, c], axis=-1)
    return np.stack([real, imag], axis=1).reshape(256, 512).astype(ml_dtypes.bfloat16)


def inverse_table():
    g, q = np.meshgrid(np.arange(GROUP), np.arange(QUADS), indexing="ij")
    k2 = (16 * q + g).reshape(-1)
    angle = 2.0 * np.pi * (np.outer(k2, np.arange(SHORT)) % SHORT) / SHORT
    c, s = np.cos(angle), np.sin(angle)
    real = np.concatenate([c, s], axis=1)
    imag = np.concatenate([-s, c], axis=1)
    return np.concatenate([real, imag], axis=0).astype(ml_dtypes.bfloat16)


def beam_table():
    feed = np.arange(FEEDS)
    angle = 2.0 * np.pi * (np.outer(feed, feed) % FEEDS) / FEEDS
    c = np.cos(angle).astype(np.float32).astype(ml_dtypes.bfloat16).astype(np.float32)
    s = np.sin(angle).astype(np.float32).astype(ml_dtypes.bfloat16).astype(np.float32)
    real = np.concatenate([c.T, s.T], axis=1)
    imag = np.concatenate([-s.T, c.T], axis=1)
    both = np.stack([real, imag], axis=1).reshape(32, 4, 2, 2, 512).transpose(1, 0, 2, 3, 4)
    return (both.reshape(512, 512) / 16.0).astype(ml_dtypes.bfloat16)


def spacing_rows():
    g = np.arange(GROUP)[:, None, None, None]
    k1 = np.arange(8)[None, None, :, None]
    q = np.arange(QUADS)[None, None, None, :]
    k = (128 * q + 8 * g + k1 + np.zeros((1, 2, 1, 1), np.int64)).astype(np.float32)
    base = np.float32(1.0) + k / np.float32(1024.0)
    rows = (np.float32(1.0) / (base * base)).reshape(GROUP, 128).astype(np.float32)
    return np.stack([np.roll(rows[i], 8 * i) for i in range(GROUP)])


def swap(low, high, axis, by):
    rank = low.ndim
    index = lax.broadcasted_iota(jnp.int32, low.shape, rank - 2 + axis)
    first = (index & by) == 0
    size = low.shape[rank - 2 + axis]
    if axis == 1:
        flat = (-1, low.shape[-1])
        up = pltpu.roll(high.reshape(flat), by, 1).reshape(low.shape)
        down = pltpu.roll(low.reshape(flat), size - by, 1).reshape(low.shape)
    else:
        up = pltpu.roll(high, by, rank - 2)
        down = pltpu.roll(low, size - by, rank - 2)
    return jnp.where(first, low, up), jnp.where(first, down, high)


def gather(parts, lane):
    n = len(parts)
    index = lax.broadcasted_iota(jnp.int32, parts[0].shape, 1)
    by = 1
    while by < n:
        here = (index & (by * lane)) == 0
        parts = [jnp.where(here, parts[i], parts[(i + by) % n]) for i in range(n)]
        by *= 2
    return [pltpu.roll(parts[(n - k) % n], (n - k) * lane, 1) if k else parts[0] for k in range(n)]


def eight_forward(x):
    s04, d04, s26, d26 = x[0] + x[4], x[0] - x[4], x[2] + x[6], x[2] - x[6]
    s15, d15, s37, d37 = x[1] + x[5], x[1] - x[5], x[3] + x[7], x[3] - x[7]
    even, odd = s04 + s26, s15 + s37
    near, far = HALF_ROOT * (d15 - d37), HALF_ROOT * (d15 + d37)
    y1 = (d04 + near, -(d26 + far))
    y2 = (s04 - s26, s37 - s15)
    y3 = (d04 - near, d26 - far)
    return (even + odd, None), y1, y2, y3, (even - odd, None)


def eight_inverse(a0, a1, a2, a3, a4, b1, b2, b3):
    plus, minus = a0 + a4, a0 - a4
    a13, a31 = a1 + a3, HALF_ROOT * (a1 - a3)
    b13, b31 = HALF_ROOT * (b1 + b3), b1 - b3
    o0, o2 = plus + a2, plus - a2
    m1, m3 = minus - b2, minus + b2
    return (
        o0 + a13, m1 + a31 - b13, o2 - b31, m3 - a31 - b13,
        o0 - a13, m1 - a31 + b13, o2 + b31, m3 + a31 + b13,
    )


def turned_phase(turns):
    return jnp.cos(turns), jnp.sin(turns)


def kernel(
    volt, gain, disp, window, twid, fwd, inv, beam, space, out,
    xv, xh, gv, wv, tv, fv, iv, bv, sv, gb, gr, gt, zs, ab, ra, xs, xb, sb, sr, ct, vs, ys, wf, wb, wr, ov,
    load_sem, out_sem, send_sem, recv_sem, hist_sem, chan_sem, beam_sem, fut_sem,
):
    me, tm = lax.axis_index("turn"), lax.axis_index("tm")
    base, g = (me // GROUP) * GROUP, me % GROUP
    xz, y = me // 4, me % 4
    after, before = (tm + 1) % 4, (tm + 3) % 4

    barrier = pltpu.get_barrier_semaphore()

    def greet_group(i, _):
        pl.semaphore_signal(barrier, inc=1, device_id={"turn": base + (g + i) % GROUP}, device_id_type=MESH)
        return 0

    def greet_quads(i, _):
        pl.semaphore_signal(barrier, inc=1, device_id={"turn": (me + GROUP * i) % 128}, device_id_type=MESH)
        return 0

    for other in (after, before):
        pl.semaphore_signal(barrier, inc=1, device_id={"tm": other}, device_id_type=MESH)
    lax.fori_loop(1, QUADS, greet_quads, 0)
    lax.fori_loop(1, GROUP, greet_group, 0)

    loads = [
        pltpu.make_async_copy(a, b, load_sem.at[i])
        for i, (a, b) in enumerate(
            [(volt, xv), (gain, gv), (window, wv), (twid, tv), (fwd, fv), (inv, iv), (beam, bv), (space, sv)]
        )
    ]
    for load in loads:
        load.start()
    loads[0].wait()
    loads[1].wait()
    gb[...] = gv[...].reshape(16, 2048).astype(BF16)
    pl.semaphore_wait(barrier, 2 + QUADS - 1 + GROUP - 1)

    history = [
        pltpu.make_async_remote_copy(
            src_ref=xv.at[:, pl.ds((slot + 1) * NFFT, NFFT)], dst_ref=xh.at[slot],
            send_sem=hist_sem.at[0, slot], recv_sem=hist_sem.at[1, slot],
            device_id={"tm": after}, device_id_type=MESH,
        )
        for slot in range(3)
    ]
    for slot in (2, 1, 0):
        history[slot].start()

    for i in (2, 3, 4):
        loads[i].wait()
    keep = jnp.where(tm > 0, 1.0, 0.0).astype(F32)

    def frame_of(at):
        if at < 0:
            return xh[at + 3].astype(F32) * keep
        return xv[:, pl.ds(at * NFFT, NFFT)].astype(F32)

    def channelize(f):
        total = wv[0:1, :] * frame_of(f - 3)
        for p in range(1, TAPS):
            total = total + wv[p : p + 1, :] * frame_of(f - 3 + p)
        total = total.astype(BF16).astype(F32)
        parts = eight_forward([total[:, n * SHORT : (n + 1) * SHORT] for n in range(8)])
        for k1 in range(8):
            re, im = parts[k1] if k1 < 5 else parts[8 - k1]
            c, s = tv[k1, 0:1, :], -tv[k1, 1:2, :]
            if im is None:
                zr, zi = re * c, re * s
            elif k1 < 5:
                zr, zi = re * c - im * s, re * s + im * c
            else:
                zr, zi = re * c + im * s, re * s - im * c
            rows = pl.ds(pl.multiple_of((k1 + g) % 8 * 16, 16), 16)
            zs[f, rows, 0:SHORT] = zr.astype(BF16)
            zs[f, rows, SHORT : 2 * SHORT] = zi.astype(BF16)

    contract = (((1,), (1,)), ((), ()))

    def exchange_channels(f):
        channels = lax.dot_general(fv[...], zs[f], contract, preferred_element_type=F32)
        ab[f] = channels.reshape(GROUP, 16, 128).astype(BF16)

        def send_channels(i, _):
            to = (g + i) % GROUP
            pltpu.make_async_remote_copy(
                src_ref=ab.at[f, to], dst_ref=ra.at[f, g],
                send_sem=send_sem.at[1], recv_sem=chan_sem.at[f],
                device_id={"turn": base + to}, device_id_type=MESH,
            ).start()
            return 0

        lax.fori_loop(1, GROUP, send_channels, 0)
        ra[f, g] = ab[f, g]

    channelize(3)
    exchange_channels(3)

    mine = me // GROUP

    def send_gain(i, _):
        q = (mine + i) % QUADS
        pltpu.make_async_remote_copy(
            src_ref=gb.at[:, pl.ds(pl.multiple_of(q * FEEDS, FEEDS), FEEDS)], dst_ref=gr.at[mine],
            send_sem=send_sem.at[0], recv_sem=recv_sem.at[0],
            device_id={"turn": q * GROUP + g}, device_id_type=MESH,
        ).start()
        return 0

    lax.fori_loop(1, QUADS, send_gain, 0)
    gr[mine] = gb[:, pl.ds(pl.multiple_of(mine * FEEDS, FEEDS), FEEDS)]

    for f in (2, 1, 0):
        history[f].wait_recv()
        channelize(f)
        exchange_channels(f)

    pltpu.make_async_copy(gr.at[pl.ds(0, QUADS - 1)], gr.at[pl.ds(0, QUADS - 1)], recv_sem.at[0]).wait()
    for half in range(2):
        got = gr[:, :, half * 128 : (half + 1) * 128].astype(F32).reshape(QUADS, 2, 8, 128)
        for b in range(3):
            split = got.reshape(2 ** (2 - b), 2, 2**b, 2, 8, 128)
            flat = (-1, 8, 128)
            low, high = swap(split[:, 0].reshape(flat), split[:, 1].reshape(flat), 0, 1 << b)
            part = (2 ** (2 - b), 2**b, 2, 8, 128)
            got = jnp.stack([low.reshape(part), high.reshape(part)], axis=1).reshape(QUADS, 2, 8, 128)
        gt[half] = got

    loads[6].wait()
    loads[5].wait()
    for f in (3, 2, 1, 0):
        pltpu.make_async_copy(ra.at[f, pl.ds(0, GROUP - 1)], ra.at[f, pl.ds(0, GROUP - 1)], chan_sem.at[f]).wait()
        for half in range(2):
            items = gather([ra[f, half * 8 + i].astype(F32) for i in range(8)], 16)
            for k1 in range(8):
                re, im = items[k1][:8], items[k1][8:]
                gre, gim = gt[half, k1, 0], gt[half, k1, 1]
                rows = pl.ds(pl.multiple_of((f // 2) * 128 + ((f % 2) * 8 + k1 + g) % 16 * 8, 8), 8)
                xs[rows, half * 128 : (half + 1) * 128] = gre * re - gim * im
                xs[rows, FEEDS + half * 128 : FEEDS + (half + 1) * 128] = gre * im + gim * re
    xb[...] = xs[...].astype(BF16)

    row3 = lax.broadcasted_iota(jnp.int32, (16, 8, 128), 1)
    xh_me, z_me = me // 64, xz % 16
    for pair in range(2):
        for c in (2 * pair, 2 * pair + 1):
            to_y = (y + c) % 4
            both = lax.dot_general(
                bv[pl.ds(pl.multiple_of(to_y * 128, 128), 128), :], xb[...], contract, preferred_element_type=F32
            )
            low, high = both[:, :128].reshape(16, 8, 128), both[:, 128:].reshape(16, 8, 128)
            sb[to_y, :, 0] = jnp.where(row3 < 4, low, pltpu.roll(high, 4, 1)).astype(BF16)
            sb[to_y, :, 1] = jnp.where(row3 < 4, pltpu.roll(low, 4, 1), high).astype(BF16)

        def send_beams(c, x_by, z_by):
            to_y = (y + c) % 4
            to = ((xh_me + x_by) % 2) * 16 + (z_me + z_by) % 16
            pltpu.make_async_remote_copy(
                src_ref=sb.at[to_y, to // 2, to % 2], dst_ref=sr.at[me],
                send_sem=send_sem.at[2], recv_sem=beam_sem.at[c],
                device_id={"turn": to * 4 + to_y}, device_id_type=MESH,
            ).start()

        def send_far(i, _):
            z_by = 8 + (1 - 2 * (i % 2)) * ((i + 1) // 2)
            for c in (2 * pair, 2 * pair + 1):
                for x_by in range(2):
                    send_beams(c, x_by, z_by)
            return 0

        lax.fori_loop(0, 15, send_far, 0)
        for c in (2 * pair, 2 * pair + 1):
            for x_by in range(2):
                if c + x_by > 0:
                    send_beams(c, x_by, 0)
    sr[me] = sb[y, xz // 2, xz % 2]

    loads[7].wait()
    row = lax.broadcasted_iota(jnp.int32, (8, 128), 0)

    def phases(at, _):
        for e in range(4):
            scale = jnp.where((row & 2) == 0, disp[e], disp[4 + e])
            c, s = turned_phase(scale * sv[pl.ds(at, 1), :])
            ct[at, 0, e] = 0.5 * c
            ct[at, 1, e] = 0.5 * s
        return 0

    lax.fori_loop(0, GROUP, phases, 0)

    def east_west(zl, from_y):
        at = zl * 4 + from_y
        ns = [[None] * 4, [None] * 4]
        for c in range(4):
            one = sr[c * GROUP + at].astype(F32)
            two = sr[64 + c * GROUP + at].astype(F32)
            ns[0][c], ns[1][c] = swap(one, two, 0, 1)
        (r0, r1, r2, r3), (i0, i1, i2, i3) = ns
        ra_, rb_, rc_, rd_ = r0 + r2, r0 - r2, r1 + r3, r1 - r3
        ia_, ib_, ic_, id_ = i0 + i2, i0 - i2, i1 + i3, i1 - i3
        beams = [(ra_ + rc_, ia_ + ic_), (rb_ + id_, ib_ - rd_), (ra_ - rc_, ia_ - ic_), (rb_ - id_, ib_ + rd_)]
        chirped = []
        for e in range(4):
            re, im = beams[e]
            c, s = ct[at, 0, e], ct[at, 1, e]
            chirped.append((re * c - im * s, re * s + im * c))
        for high in range(2):
            for r in range(2):
                first, second = swap(chirped[2 * high][r], chirped[2 * high + 1][r], 0, 4)
                vs[r, 0, at, 8 * high : 8 * high + 8] = first
                vs[r, 1, at, 8 * high : 8 * high + 8] = second
        return from_y

    for c in range(4):
        count = 32 if c else 31
        pltpu.make_async_copy(sr.at[pl.ds(0, count)], sr.at[pl.ds(0, count)], beam_sem.at[c]).wait()
        lax.fori_loop(0, 4, east_west, (y + 4 - c) % 4)

    for r in range(2):
        for h in range(2):
            items = gather([vs[r, h, i] for i in range(GROUP)], 8)
            for k in range(GROUP):
                ys[2 * h + k // 8, k % 8, :, r * 128 : (r + 1) * 128] = items[k].astype(BF16)

    def synthesise(f):
        z = jnp.dot(ys[f].reshape(128, 256), iv[...], preferred_element_type=F32).reshape(8, 16, 512)
        re, im = [], []
        for k1 in range(8):
            zr, zi = z[k1, :, :SHORT], z[k1, :, SHORT:]
            c, s = tv[k1, 0:1, :], tv[k1, 1:2, :]
            re.append(zr * c - zi * s)
            im.append(zr * s + zi * c if k1 % 4 else None)
        outs = eight_inverse(
            re[0], re[1] + re[7], re[2] + re[6], re[3] + re[5], re[4],
            im[1] - im[7], im[2] - im[6], im[3] - im[5],
        )
        for n in range(8):
            wf[f, :, n * SHORT : (n + 1) * SHORT] = outs[n]
            if f < 3:
                wb[f, :, n * SHORT : (n + 1) * SHORT] = outs[n].astype(BF16)

    future = [
        pltpu.make_async_remote_copy(
            src_ref=wb.at[f], dst_ref=wr.at[f], send_sem=fut_sem.at[0, f], recv_sem=fut_sem.at[1, f],
            device_id={"tm": before}, device_id_type=MESH,
        )
        for f in range(3)
    ]
    for f in range(3):
        synthesise(f)
        future[f].start()
    synthesise(3)

    last = jnp.where(tm < 3, 1.0, 0.0).astype(F32)

    def store_frame(f):
        store = pltpu.make_async_copy(
            ov.at[:, pl.ds(f * NFFT, NFFT)], out.at[:, pl.ds(f * NFFT, NFFT)], out_sem.at[f]
        )
        store.start()
        return store

    for f in range(FRAMES):
        total = wv[3:4, :] * wf[f]
        for p in range(1, FRAMES - f):
            total = total + wv[3 - p : 4 - p, :] * wf[f + p]
        ov[:, f * NFFT : (f + 1) * NFFT] = total
    stores = [store_frame(0)]
    for f in range(1, FRAMES):
        future[f - 1].wait_recv()
        total = ov[:, f * NFFT : (f + 1) * NFFT]
        for p in range(FRAMES - f, TAPS):
            total = total + (wv[3 - p : 4 - p, :] * last) * wr[f + p - 4].astype(F32)
        ov[:, f * NFFT : (f + 1) * NFFT] = total
        stores.append(store_frame(f))

    for copy in history + future:
        copy.wait_send()
    pltpu.make_async_copy(gr.at[pl.ds(0, QUADS - 1)], gr.at[pl.ds(0, QUADS - 1)], send_sem.at[0]).wait()
    for f in range(FRAMES):
        pltpu.make_async_copy(ra.at[f, pl.ds(0, GROUP - 1)], ra.at[f, pl.ds(0, GROUP - 1)], send_sem.at[1]).wait()
    pltpu.make_async_copy(sr.at[pl.ds(0, 127)], sr.at[pl.ds(0, 127)], send_sem.at[2]).wait()
    for store in stores:
        store.wait()


def body(voltages, gains, dispersion):
    anywhere = pl.BlockSpec(memory_space=pl.ANY)
    vmem = pltpu.VMEM
    rows = pl.pallas_call(
        kernel,
        out_shape=jax.ShapeDtypeStruct((16, FRAMES * NFFT), F32),
        in_specs=[anywhere, anywhere, pl.BlockSpec(memory_space=pltpu.SMEM)] + [anywhere] * 6,
        out_specs=anywhere,
        scratch_shapes=[
            vmem((16, FRAMES * NFFT), BF16),
            vmem((3, 16, NFFT), BF16),
            vmem((2, 8, 2048), F32),
            vmem((TAPS, NFFT), F32),
            vmem((8, 2, SHORT), F32),
            vmem((256, 512), BF16),
            vmem((256, 512), BF16),
            vmem((512, 512), BF16),
            vmem((GROUP, 128), F32),
            vmem((16, 2048), BF16),
            vmem((QUADS, 16, FEEDS), BF16),
            vmem((2, 8, 2, 8, 128), F32),
            vmem((FRAMES, 128, 512), BF16),
            vmem((FRAMES, GROUP, 16, 128), BF16),
            vmem((FRAMES, GROUP, 16, 128), BF16),
            vmem((256, 512), F32),
            vmem((256, 512), BF16),
            vmem((4, 16, 2, 8, 128), BF16),
            vmem((128, 8, 128), BF16),
            vmem((GROUP, 2, 4, 8, 128), F32),
            vmem((2, 2, GROUP, 16, 128), F32),
            vmem((FRAMES, 8, 16, 256), BF16),
            vmem((FRAMES, 16, NFFT), F32),
            vmem((3, 16, NFFT), BF16),
            vmem((3, 16, NFFT), BF16),
            vmem((16, FRAMES * NFFT), F32),
            pltpu.SemaphoreType.DMA((8,)),
            pltpu.SemaphoreType.DMA((FRAMES,)),
            pltpu.SemaphoreType.DMA((3,)),
            pltpu.SemaphoreType.DMA((1,)),
            pltpu.SemaphoreType.DMA((2, 3)),
            pltpu.SemaphoreType.DMA((FRAMES,)),
            pltpu.SemaphoreType.DMA((4,)),
            pltpu.SemaphoreType.DMA((2, 3)),
        ],
        compiler_params=pltpu.CompilerParams(
            collective_id=0, has_side_effects=True, vmem_limit_bytes=60 * 1024 * 1024
        ),
        cost_estimate=pl.CostEstimate(flops=500_000_000, bytes_accessed=3_000_000, transcendentals=0),
    )(
        voltages, gains.transpose(0, 2, 1), dispersion,
        window_rows(), twiddle_rows(), forward_table(), inverse_table(), beam_table(), spacing_rows(),
    )
    ordered = rows.reshape(4, 2, 2, FRAMES * NFFT).transpose(1, 0, 2, 3)
    return ordered.reshape(8, 2, FRAMES * NFFT)


def solution(mesh):
    placed = (P("turn", "tm"), P(None, None, "turn"), P("turn"))
    return jax.shard_map(
        body, mesh=mesh, in_specs=placed, out_specs=P("turn", None, "tm"), check_vma=False
    )
```

```python
import functools
import math

import jax
import jax.numpy as jnp
import ml_dtypes
import numpy as np
from jax import lax
from jax.experimental import pallas as pl
from jax.experimental.pallas import tpu as pltpu
from jax.sharding import PartitionSpec as P

NFFT = 2048
TAPS = 4
FRAMES = 4
GROUP = 16
QUADS = 8
FEEDS = 256
SHORT = 256
BF16 = jnp.bfloat16
F32 = jnp.float32
MESH = pl.DeviceIdType.MESH
HALF_ROOT = math.sqrt(0.5)


def window_rows():
    extent = TAPS * NFFT
    t = np.arange(extent, dtype=np.float64) + 0.5
    shape = np.sinc((t - 0.5 * extent) / NFFT) * (0.5 - 0.5 * np.cos(t * (2.0 * np.pi / extent)))
    return shape.reshape(TAPS, NFFT).astype(np.float32)


def twiddle_rows():
    angle = 2.0 * np.pi * np.outer(np.arange(8), np.arange(SHORT)) / NFFT
    return (np.stack([np.cos(angle), np.sin(angle)], axis=1) / math.sqrt(NFFT)).astype(np.float32)


def forward_table():
    g, q = np.meshgrid(np.arange(GROUP), np.arange(QUADS), indexing="ij")
    k2 = 16 * q + g
    angle = 2.0 * np.pi * (k2[:, :, None] * np.arange(SHORT) % SHORT) / SHORT
    c, s = np.cos(angle), np.sin(angle)
    real = np.concatenate([c, s], axis=-1)
    imag = np.concatenate([-s, c], axis=-1)
    return np.stack([real, imag], axis=1).reshape(256, 512).astype(ml_dtypes.bfloat16)


def inverse_table():
    g, q = np.meshgrid(np.arange(GROUP), np.arange(QUADS), indexing="ij")
    k2 = (16 * q + g).reshape(-1)
    angle = 2.0 * np.pi * (np.outer(k2, np.arange(SHORT)) % SHORT) / SHORT
    c, s = np.cos(angle), np.sin(angle)
    real = np.concatenate([c, s], axis=1)
    imag = np.concatenate([-s, c], axis=1)
    return np.concatenate([real, imag], axis=0).astype(ml_dtypes.bfloat16)


def beam_table():
    feed = np.arange(FEEDS)
    angle = 2.0 * np.pi * (np.outer(feed, feed) % FEEDS) / FEEDS
    c = np.cos(angle).astype(np.float32).astype(ml_dtypes.bfloat16).astype(np.float32)
    s = np.sin(angle).astype(np.float32).astype(ml_dtypes.bfloat16).astype(np.float32)
    real = np.concatenate([c.T, s.T], axis=1)
    imag = np.concatenate([-s.T, c.T], axis=1)
    both = np.stack([real, imag], axis=1).reshape(32, 4, 2, 2, 512).transpose(1, 0, 2, 3, 4)
    return (both.reshape(512, 512) / 16.0).astype(ml_dtypes.bfloat16)


def spacing_rows():
    g = np.arange(GROUP)[:, None, None, None]
    k1 = np.arange(8)[None, None, :, None]
    q = np.arange(QUADS)[None, None, None, :]
    k = (128 * q + 8 * g + k1 + np.zeros((1, 2, 1, 1), np.int64)).astype(np.float32)
    base = np.float32(1.0) + k / np.float32(1024.0)
    rows = (np.float32(1.0) / (base * base)).reshape(GROUP, 128).astype(np.float32)
    return np.stack([np.roll(rows[i], 8 * i) for i in range(GROUP)])


def swap(low, high, axis, by):
    rank = low.ndim
    index = lax.broadcasted_iota(jnp.int32, low.shape, rank - 2 + axis)
    first = (index & by) == 0
    size = low.shape[rank - 2 + axis]
    if axis == 1:
        flat = (-1, low.shape[-1])
        up = pltpu.roll(high.reshape(flat), by, 1).reshape(low.shape)
        down = pltpu.roll(low.reshape(flat), size - by, 1).reshape(low.shape)
    else:
        up = pltpu.roll(high, by, rank - 2)
        down = pltpu.roll(low, size - by, rank - 2)
    return jnp.where(first, low, up), jnp.where(first, down, high)


def gather(parts, lane):
    n = len(parts)
    index = lax.broadcasted_iota(jnp.int32, parts[0].shape, 1)
    by = 1
    while by < n:
        here = (index & (by * lane)) == 0
        parts = [jnp.where(here, parts[i], parts[(i + by) % n]) for i in range(n)]
        by *= 2
    return [pltpu.roll(parts[(n - k) % n], (n - k) * lane, 1) if k else parts[0] for k in range(n)]


def eight_forward(x):
    s04, d04, s26, d26 = x[0] + x[4], x[0] - x[4], x[2] + x[6], x[2] - x[6]
    s15, d15, s37, d37 = x[1] + x[5], x[1] - x[5], x[3] + x[7], x[3] - x[7]
    even, odd = s04 + s26, s15 + s37
    near, far = HALF_ROOT * (d15 - d37), HALF_ROOT * (d15 + d37)
    y1 = (d04 + near, -(d26 + far))
    y2 = (s04 - s26, s37 - s15)
    y3 = (d04 - near, d26 - far)
    return (even + odd, None), y1, y2, y3, (even - odd, None)


def eight_inverse(a0, a1, a2, a3, a4, b1, b2, b3):
    plus, minus = a0 + a4, a0 - a4
    a13, a31 = a1 + a3, HALF_ROOT * (a1 - a3)
    b13, b31 = HALF_ROOT * (b1 + b3), b1 - b3
    o0, o2 = plus + a2, plus - a2
    m1, m3 = minus - b2, minus + b2
    return (
        o0 + a13, m1 + a31 - b13, o2 - b31, m3 - a31 - b13,
        o0 - a13, m1 - a31 + b13, o2 + b31, m3 + a31 + b13,
    )


def turned_phase(turns):
    return jnp.cos(turns), jnp.sin(turns)


def kernel(
    volt, gain, disp, window, twid, fwd, inv, beam, space, out,
    xv, xh, gv, wv, tv, fv, iv, bv, sv, gb, gr, gt, zs, al, rl, ab, ra, xs, xb, sb, sr, ct, vs, ys, wf, wb, wr, ov,
    load_sem, out_sem, send_sem, recv_sem, hist_sem, chan_sem, beam_sem, fut_sem,
):
    me, tm = lax.axis_index("turn"), lax.axis_index("tm")
    mine, g = lax.div(me, GROUP), lax.rem(me, GROUP)
    base = mine * GROUP
    xz, y = lax.div(me, 4), lax.rem(me, 4)
    after, before = lax.rem(tm + 1, 4), lax.rem(tm + 3, 4)

    barrier = pltpu.get_barrier_semaphore()

    def greet_group(i, _):
        pl.semaphore_signal(barrier, inc=1, device_id={"turn": base + lax.rem(g + i, GROUP)}, device_id_type=MESH)
        return 0

    def greet_quads(i, _):
        pl.semaphore_signal(barrier, inc=1, device_id={"turn": lax.rem(me + GROUP * i, 128)}, device_id_type=MESH)
        return 0

    lax.fori_loop(1, QUADS, greet_quads, 0)
    for other in (after, before):
        pl.semaphore_signal(barrier, inc=1, device_id={"tm": other}, device_id_type=MESH)
    lax.fori_loop(1, GROUP, greet_group, 0)

    loads = [
        pltpu.make_async_copy(a, b, load_sem.at[i])
        for i, (a, b) in enumerate(
            [(volt, xv), (gain, gv), (window, wv), (twid, tv), (fwd, fv), (inv, iv), (beam, bv), (space, sv)]
        )
    ]
    for load in loads:
        load.start()
    loads[0].wait()
    loads[1].wait()
    gb[...] = gv[...].reshape(16, 2048).astype(BF16)
    pl.semaphore_wait(barrier, 2 + QUADS - 1 + GROUP - 1)


    def send_gain(i, _):
        q = lax.rem(mine + i, QUADS)
        pltpu.make_async_remote_copy(
            src_ref=gb.at[:, pl.ds(pl.multiple_of(q * FEEDS, FEEDS), FEEDS)], dst_ref=gr.at[mine],
            send_sem=send_sem.at[0], recv_sem=recv_sem.at[0],
            device_id={"turn": q * GROUP + g}, device_id_type=MESH,
        ).start()
        return 0

    lax.fori_loop(1, QUADS, send_gain, 0)
    gr[mine] = gb[:, pl.ds(pl.multiple_of(mine * FEEDS, FEEDS), FEEDS)]

    history = [
        pltpu.make_async_remote_copy(
            src_ref=xv.at[:, pl.ds((slot + 1) * NFFT, NFFT)], dst_ref=xh.at[slot],
            send_sem=hist_sem.at[0, slot], recv_sem=hist_sem.at[1, slot],
            device_id={"tm": after}, device_id_type=MESH,
        )
        for slot in range(3)
    ]
    for slot in (2, 1, 0):
        history[slot].start()

    for i in (2, 3, 4):
        loads[i].wait()
    keep = jnp.where(tm > 0, 1.0, 0.0).astype(F32)

    def frame_of(at):
        if at < 0:
            return xh[at + 3].astype(F32) * keep
        return xv[:, pl.ds(at * NFFT, NFFT)].astype(F32)

    def channelize(f):
        total = wv[0:1, :] * frame_of(f - 3)
        for p in range(1, TAPS):
            total = total + wv[p : p + 1, :] * frame_of(f - 3 + p)
        total = total.astype(BF16).astype(F32)
        parts = eight_forward([total[:, n * SHORT : (n + 1) * SHORT] for n in range(8)])
        for k1 in range(8):
            re, im = parts[k1] if k1 < 5 else parts[8 - k1]
            c, s = tv[k1, 0:1, :], -tv[k1, 1:2, :]
            if im is None:
                zr, zi = re * c, re * s
            elif k1 < 5:
                zr, zi = re * c - im * s, re * s + im * c
            else:
                zr, zi = re * c + im * s, re * s - im * c
            rows = pl.ds(pl.multiple_of(lax.rem(k1 + g, 8) * 16, 16), 16)
            zs[f, rows, 0:SHORT] = zr.astype(BF16)
            zs[f, rows, SHORT : 2 * SHORT] = zi.astype(BF16)

    contract = (((1,), (1,)), ((), ()))

    def transform(f):
        channels = lax.dot_general(fv[...], zs[f], contract, preferred_element_type=F32)
        return channels.reshape(GROUP, 16, 128).astype(BF16)

    def exchange_channels(part, source, target):
        def send_channels(i, _):
            to = lax.rem(g + i, GROUP)
            pltpu.make_async_remote_copy(
                src_ref=source.at[to], dst_ref=target.at[g],
                send_sem=chan_sem.at[0, part], recv_sem=chan_sem.at[1, part],
                device_id={"turn": base + to}, device_id_type=MESH,
            ).start()
            return 0

        lax.fori_loop(1, GROUP, send_channels, 0)
        target[g] = source[g]

    channelize(3)
    al[...] = transform(3)
    exchange_channels(0, al, rl)

    for f in (2, 1, 0):
        history[f].wait_recv()
        channelize(f)
        ab[:, f] = transform(f)
    exchange_channels(1, ab, ra)

    pltpu.make_async_copy(gr.at[pl.ds(0, QUADS - 1)], gr.at[pl.ds(0, QUADS - 1)], recv_sem.at[0]).wait()
    for half in range(2):
        got = gr[:, :, half * 128 : (half + 1) * 128].astype(F32).reshape(QUADS, 2, 8, 128)
        for b in range(3):
            split = got.reshape(2 ** (2 - b), 2, 2**b, 2, 8, 128)
            flat = (-1, 8, 128)
            low, high = swap(split[:, 0].reshape(flat), split[:, 1].reshape(flat), 0, 1 << b)
            part = (2 ** (2 - b), 2**b, 2, 8, 128)
            got = jnp.stack([low.reshape(part), high.reshape(part)], axis=1).reshape(QUADS, 2, 8, 128)
        gt[half] = got

    loads[6].wait()
    loads[5].wait()
    turned_rows = [lax.rem(g + i, 16) * 8 for i in range(16)]
    for f in (3, 2, 1, 0):
        if f >= 2:
            arrived = rl if f == 3 else ra
            rest = arrived.at[pl.ds(0, GROUP - 1)]
            pltpu.make_async_copy(rest, rest, chan_sem.at[1, 3 - f]).wait()
        for half in range(2):
            items = [half * 8 + i for i in range(8)]
            items = [(rl[i] if f == 3 else ra[i, f]).astype(F32) for i in items]
            items = gather(items, 16)
            for k1 in range(8):
                re, im = items[k1][:8], items[k1][8:]
                gre, gim = gt[half, k1, 0], gt[half, k1, 1]
                rows = pl.ds(pl.multiple_of((f // 2) * 128 + turned_rows[(f % 2) * 8 + k1], 8), 8)
                xs[rows, half * 128 : (half + 1) * 128] = gre * re - gim * im
                xs[rows, FEEDS + half * 128 : FEEDS + (half + 1) * 128] = gre * im + gim * re
    xb[...] = xs[...].astype(BF16)

    row3 = lax.broadcasted_iota(jnp.int32, (16, 8, 128), 1)
    x_me, z_me = lax.div(me, 64), lax.rem(xz, 16)
    x_at, y_at = [x_me * 16, 16 - x_me * 16], [lax.rem(y + c, 4) for c in range(4)]
    for pair in range(2):
        for c in (2 * pair, 2 * pair + 1):
            to_y = y_at[c]
            both = lax.dot_general(
                bv[pl.ds(pl.multiple_of(to_y * 128, 128), 128), :], xb[...], contract, preferred_element_type=F32
            )
            low, high = both[:, :128].reshape(16, 8, 128), both[:, 128:].reshape(16, 8, 128)
            even = jnp.where(row3 < 4, low, pltpu.roll(high, 4, 1))
            odd = jnp.where(row3 < 4, pltpu.roll(low, 4, 1), high)
            sb[to_y] = jnp.stack([even, odd], axis=1).reshape(32, 8, 128).astype(BF16)

        def send_beams(c, x_by, z_to):
            to_y = y_at[c]
            to = x_at[x_by] + z_to
            pltpu.make_async_remote_copy(
                src_ref=sb.at[to_y, to], dst_ref=sr.at[me],
                send_sem=send_sem.at[2], recv_sem=beam_sem.at[c],
                device_id={"turn": to * 4 + to_y}, device_id_type=MESH,
            ).start()

        def send_far(i, _):
            z_to = lax.rem(z_me + 8 + (1 - 2 * lax.rem(i, 2)) * lax.div(i + 1, 2), 16)
            for c in (2 * pair, 2 * pair + 1):
                for x_by in range(2):
                    send_beams(c, x_by, z_to)
            return 0

        lax.fori_loop(0, 15, send_far, 0)
        for c in (2 * pair, 2 * pair + 1):
            for x_by in range(2):
                if c + x_by > 0:
                    send_beams(c, x_by, z_me)
    sr[me] = sb[y, xz]

    loads[7].wait()
    row = lax.broadcasted_iota(jnp.int32, (8, 128), 0)

    def phases(at, _):
        for e in range(4):
            scale = jnp.where((row & 2) == 0, disp[e], disp[4 + e])
            c, s = turned_phase(scale * sv[pl.ds(at, 1), :])
            ct[at, 0, e] = 0.5 * c
            ct[at, 1, e] = 0.5 * s
        return 0

    lax.fori_loop(0, GROUP, phases, 0)

    def east_west(zl, from_y):
        at = zl * 4 + from_y
        ns = [[None] * 4, [None] * 4]
        for c in range(4):
            one = sr[c * GROUP + at].astype(F32)
            two = sr[64 + c * GROUP + at].astype(F32)
            ns[0][c], ns[1][c] = swap(one, two, 0, 1)
        (r0, r1, r2, r3), (i0, i1, i2, i3) = ns
        ra_, rb_, rc_, rd_ = r0 + r2, r0 - r2, r1 + r3, r1 - r3
        ia_, ib_, ic_, id_ = i0 + i2, i0 - i2, i1 + i3, i1 - i3
        beams = [(ra_ + rc_, ia_ + ic_), (rb_ + id_, ib_ - rd_), (ra_ - rc_, ia_ - ic_), (rb_ - id_, ib_ + rd_)]
        chirped = []
        for e in range(4):
            re, im = beams[e]
            c, s = ct[at, 0, e], ct[at, 1, e]
            chirped.append((re * c - im * s, re * s + im * c))
        for r in range(2):
            even = swap(chirped[0][r], chirped[2][r], 0, 4)
            odd = swap(chirped[1][r], chirped[3][r], 0, 4)
            for h in range(2):
                first, second = swap(even[h], odd[h], 0, 2)
                vs[r, h, at, :8] = first
                vs[r, h, at, 8:] = second
        return from_y

    for c in range(4):
        count = 32 if c else 31
        pltpu.make_async_copy(sr.at[pl.ds(0, count)], sr.at[pl.ds(0, count)], beam_sem.at[c]).wait()
        lax.fori_loop(0, 4, east_west, lax.rem(y + 4 - c, 4))

    for r in range(2):
        for h in range(2):
            items = gather([vs[r, h, i] for i in range(GROUP)], 8)
            for k in range(GROUP):
                ys[2 * h + k // 8, k % 8, :, r * 128 : (r + 1) * 128] = items[k].astype(BF16)

    def synthesise(f):
        z = jnp.dot(ys[f].reshape(128, 256), iv[...], preferred_element_type=F32).reshape(8, 16, 512)
        re, im = [], []
        for k1 in range(8):
            zr, zi = z[k1, :, :SHORT], z[k1, :, SHORT:]
            c, s = tv[k1, 0:1, :], tv[k1, 1:2, :]
            re.append(zr * c - zi * s)
            im.append(zr * s + zi * c if k1 % 4 else None)
        outs = eight_inverse(
            re[0], re[1] + re[7], re[2] + re[6], re[3] + re[5], re[4],
            im[1] - im[7], im[2] - im[6], im[3] - im[5],
        )
        for n in range(8):
            wf[f, :, n * SHORT : (n + 1) * SHORT] = outs[n]
            if f < 3:
                wb[f, :, n * SHORT : (n + 1) * SHORT] = outs[n].astype(BF16)

    future = [
        pltpu.make_async_remote_copy(
            src_ref=wb.at[f], dst_ref=wr.at[f], send_sem=fut_sem.at[0, f], recv_sem=fut_sem.at[1, f],
            device_id={"tm": before}, device_id_type=MESH,
        )
        for f in range(3)
    ]
    for f in range(3):
        synthesise(f)
        future[f].start()
    synthesise(3)

    last = jnp.where(tm < 3, 1.0, 0.0).astype(F32)

    def store_frame(f):
        store = pltpu.make_async_copy(
            ov.at[:, pl.ds(f * NFFT, NFFT)], out.at[:, pl.ds(f * NFFT, NFFT)], out_sem.at[f]
        )
        store.start()
        return store

    for f in range(FRAMES):
        total = wv[3:4, :] * wf[f]
        for p in range(1, FRAMES - f):
            total = total + wv[3 - p : 4 - p, :] * wf[f + p]
        ov[:, f * NFFT : (f + 1) * NFFT] = total
    stores = [store_frame(0)]
    for f in range(1, FRAMES):
        future[f - 1].wait_recv()
        total = ov[:, f * NFFT : (f + 1) * NFFT]
        for p in range(FRAMES - f, TAPS):
            total = total + (wv[3 - p : 4 - p, :] * last) * wr[f + p - 4].astype(F32)
        ov[:, f * NFFT : (f + 1) * NFFT] = total
        stores.append(store_frame(f))

    for copy in history + future:
        copy.wait_send()
    pltpu.make_async_copy(gr.at[pl.ds(0, QUADS - 1)], gr.at[pl.ds(0, QUADS - 1)], send_sem.at[0]).wait()
    for part, target in ((0, rl), (1, ra)):
        rest = target.at[pl.ds(0, GROUP - 1)]
        pltpu.make_async_copy(rest, rest, chan_sem.at[0, part]).wait()
    pltpu.make_async_copy(sr.at[pl.ds(0, 127)], sr.at[pl.ds(0, 127)], send_sem.at[2]).wait()
    for store in stores:
        store.wait()


def body(voltages, gains, dispersion):
    anywhere = pl.BlockSpec(memory_space=pl.ANY)
    vmem = pltpu.VMEM
    rows = pl.pallas_call(
        kernel,
        out_shape=jax.ShapeDtypeStruct((16, FRAMES * NFFT), F32),
        in_specs=[anywhere, anywhere, pl.BlockSpec(memory_space=pltpu.SMEM)] + [anywhere] * 6,
        out_specs=anywhere,
        scratch_shapes=[
            vmem((16, FRAMES * NFFT), BF16),
            vmem((3, 16, NFFT), BF16),
            vmem((2, 8, 2048), F32),
            vmem((TAPS, NFFT), F32),
            vmem((8, 2, SHORT), F32),
            vmem((256, 512), BF16),
            vmem((256, 512), BF16),
            vmem((512, 512), BF16),
            vmem((GROUP, 128), F32),
            vmem((16, 2048), BF16),
            vmem((QUADS, 16, FEEDS), BF16),
            vmem((2, 8, 2, 8, 128), F32),
            vmem((FRAMES, 128, 512), BF16),
            vmem((GROUP, 16, 128), BF16),
            vmem((GROUP, 16, 128), BF16),
            vmem((GROUP, 3, 16, 128), BF16),
            vmem((GROUP, 3, 16, 128), BF16),
            vmem((256, 512), F32),
            vmem((256, 512), BF16),
            vmem((4, 32, 8, 128), BF16),
            vmem((128, 8, 128), BF16),
            vmem((GROUP, 2, 4, 8, 128), F32),
            vmem((2, 2, GROUP, 16, 128), F32),
            vmem((FRAMES, 8, 16, 256), BF16),
            vmem((FRAMES, 16, NFFT), F32),
            vmem((3, 16, NFFT), BF16),
            vmem((3, 16, NFFT), BF16),
            vmem((16, FRAMES * NFFT), F32),
            pltpu.SemaphoreType.DMA((8,)),
            pltpu.SemaphoreType.DMA((FRAMES,)),
            pltpu.SemaphoreType.DMA((3,)),
            pltpu.SemaphoreType.DMA((1,)),
            pltpu.SemaphoreType.DMA((2, 3)),
            pltpu.SemaphoreType.DMA((2, 2)),
            pltpu.SemaphoreType.DMA((4,)),
            pltpu.SemaphoreType.DMA((2, 3)),
        ],
        compiler_params=pltpu.CompilerParams(
            collective_id=0, has_side_effects=True, vmem_limit_bytes=60 * 1024 * 1024
        ),
        cost_estimate=pl.CostEstimate(flops=500_000_000, bytes_accessed=3_000_000, transcendentals=0),
    )(
        voltages, gains.transpose(0, 2, 1), dispersion,
        window_rows(), twiddle_rows(), forward_table(), inverse_table(), beam_table(), spacing_rows(),
    )
    return rows.reshape(8, 2, FRAMES * NFFT)


def solution(mesh):
    placed = (P("turn", "tm"), P(None, None, "turn"), P("turn"))
    return jax.shard_map(
        body, mesh=mesh, in_specs=placed, out_specs=P("turn", None, "tm"), check_vma=False
    )
```

```python
import functools
import math

import jax
import jax.numpy as jnp
import ml_dtypes
import numpy as np
from jax import lax
from jax.experimental import pallas as pl
from jax.experimental.pallas import tpu as pltpu
from jax.sharding import PartitionSpec as P

NFFT = 2048
TAPS = 4
FRAMES = 4
GROUP = 16
QUADS = 8
FEEDS = 256
SHORT = 256
BF16 = jnp.bfloat16
F32 = jnp.float32
MESH = pl.DeviceIdType.MESH
HALF_ROOT = math.sqrt(0.5)


def window_rows():
    extent = TAPS * NFFT
    t = np.arange(extent, dtype=np.float64) + 0.5
    shape = np.sinc((t - 0.5 * extent) / NFFT) * (0.5 - 0.5 * np.cos(t * (2.0 * np.pi / extent)))
    return shape.reshape(TAPS, NFFT).astype(np.float32)


def twiddle_rows():
    angle = 2.0 * np.pi * np.outer(np.arange(8), np.arange(SHORT)) / NFFT
    return (np.stack([np.cos(angle), np.sin(angle)], axis=1) / math.sqrt(NFFT)).astype(np.float32)


def forward_table():
    g, q = np.meshgrid(np.arange(GROUP), np.arange(QUADS), indexing="ij")
    k2 = 16 * q + g
    angle = 2.0 * np.pi * (k2[:, :, None] * np.arange(SHORT) % SHORT) / SHORT
    c, s = np.cos(angle), np.sin(angle)
    real = np.concatenate([c, s], axis=-1)
    imag = np.concatenate([-s, c], axis=-1)
    return np.stack([real, imag], axis=1).reshape(256, 512).astype(ml_dtypes.bfloat16)


def inverse_table():
    g, q = np.meshgrid(np.arange(GROUP), np.arange(QUADS), indexing="ij")
    k2 = (16 * q + g).reshape(-1)
    angle = 2.0 * np.pi * (np.outer(k2, np.arange(SHORT)) % SHORT) / SHORT
    c, s = np.cos(angle), np.sin(angle)
    real = np.concatenate([c, s], axis=1)
    imag = np.concatenate([-s, c], axis=1)
    return np.concatenate([real, imag], axis=0).astype(ml_dtypes.bfloat16)


def beam_table():
    feed = np.arange(FEEDS)
    angle = 2.0 * np.pi * (np.outer(feed, feed) % FEEDS) / FEEDS
    c = np.cos(angle).astype(np.float32).astype(ml_dtypes.bfloat16).astype(np.float32)
    s = np.sin(angle).astype(np.float32).astype(ml_dtypes.bfloat16).astype(np.float32)
    real = np.concatenate([c.T, s.T], axis=1)
    imag = np.concatenate([-s.T, c.T], axis=1)
    both = np.stack([real, imag], axis=1).reshape(32, 4, 2, 2, 512).transpose(1, 0, 2, 3, 4)
    return (both.reshape(512, 512) / 16.0).astype(ml_dtypes.bfloat16)


def spacing_rows():
    g = np.arange(GROUP)[:, None, None, None]
    k1 = np.arange(8)[None, None, :, None]
    q = np.arange(QUADS)[None, None, None, :]
    k = (128 * q + 8 * g + k1 + np.zeros((1, 2, 1, 1), np.int64)).astype(np.float32)
    base = np.float32(1.0) + k / np.float32(1024.0)
    rows = (np.float32(1.0) / (base * base)).reshape(GROUP, 128).astype(np.float32)
    return np.stack([np.roll(rows[i], 8 * i) for i in range(GROUP)])


def swap(low, high, axis, by):
    rank = low.ndim
    index = lax.broadcasted_iota(jnp.int32, low.shape, rank - 2 + axis)
    first = (index & by) == 0
    size = low.shape[rank - 2 + axis]
    if axis == 1:
        flat = (-1, low.shape[-1])
        up = pltpu.roll(high.reshape(flat), by, 1).reshape(low.shape)
        down = pltpu.roll(low.reshape(flat), size - by, 1).reshape(low.shape)
    else:
        up = pltpu.roll(high, by, rank - 2)
        down = pltpu.roll(low, size - by, rank - 2)
    return jnp.where(first, low, up), jnp.where(first, down, high)


def gather(parts, lane):
    n = len(parts)
    index = lax.broadcasted_iota(jnp.int32, parts[0].shape, 1)
    by = 1
    while by < n:
        here = (index & (by * lane)) == 0
        parts = [jnp.where(here, parts[i], parts[(i + by) % n]) for i in range(n)]
        by *= 2
    return [pltpu.roll(parts[(n - k) % n], (n - k) * lane, 1) if k else parts[0] for k in range(n)]


def eight_forward(x):
    s04, d04, s26, d26 = x[0] + x[4], x[0] - x[4], x[2] + x[6], x[2] - x[6]
    s15, d15, s37, d37 = x[1] + x[5], x[1] - x[5], x[3] + x[7], x[3] - x[7]
    even, odd = s04 + s26, s15 + s37
    near, far = HALF_ROOT * (d15 - d37), HALF_ROOT * (d15 + d37)
    y1 = (d04 + near, -(d26 + far))
    y2 = (s04 - s26, s37 - s15)
    y3 = (d04 - near, d26 - far)
    return (even + odd, None), y1, y2, y3, (even - odd, None)


def eight_inverse(a0, a1, a2, a3, a4, b1, b2, b3):
    plus, minus = a0 + a4, a0 - a4
    a13, a31 = a1 + a3, HALF_ROOT * (a1 - a3)
    b13, b31 = HALF_ROOT * (b1 + b3), b1 - b3
    o0, o2 = plus + a2, plus - a2
    m1, m3 = minus - b2, minus + b2
    return (
        o0 + a13, m1 + a31 - b13, o2 - b31, m3 - a31 - b13,
        o0 - a13, m1 - a31 + b13, o2 + b31, m3 + a31 + b13,
    )


def kernel(
    volt, gain, disp, window, twid, fwd, inv, beam, space, out,
    xv, xh, gv, wv, tv, fv, iv, bv, sv, gb, gr, gt, zs, al, rl, ab, ra, xs, xb, sb, sr, ct, vs, ys, wf, wb, wr, pv, ov,
    load_sem, out_sem, send_sem, recv_sem, hist_sem, chan_sem, beam_sem, fut_sem,
):
    me, tm = lax.axis_index("turn"), lax.axis_index("tm")
    mine, g = lax.div(me, GROUP), lax.rem(me, GROUP)
    base = mine * GROUP
    xz, y = lax.div(me, 4), lax.rem(me, 4)
    after, before = lax.rem(tm + 1, 4), lax.rem(tm + 3, 4)

    barrier = pltpu.get_barrier_semaphore()

    def greet_group(i, _):
        pl.semaphore_signal(barrier, inc=1, device_id={"turn": base + lax.rem(g + i, GROUP)}, device_id_type=MESH)
        return 0

    def greet_quads(i, _):
        pl.semaphore_signal(barrier, inc=1, device_id={"turn": lax.rem(me + GROUP * i, 128)}, device_id_type=MESH)
        return 0

    lax.fori_loop(1, QUADS, greet_quads, 0)
    for other in (after, before):
        pl.semaphore_signal(barrier, inc=1, device_id={"tm": other}, device_id_type=MESH)
    lax.fori_loop(1, GROUP, greet_group, 0)

    loads = [
        pltpu.make_async_copy(a, b, load_sem.at[i])
        for i, (a, b) in enumerate(
            [(volt, xv), (gain, gv), (window, wv), (twid, tv), (fwd, fv), (inv, iv), (beam, bv), (space, sv)]
        )
    ]
    for load in loads:
        load.start()
    loads[0].wait()
    loads[1].wait()
    gb[...] = gv[...].reshape(16, 2048).astype(BF16)
    pl.semaphore_wait(barrier, 2 + QUADS - 1 + GROUP - 1)


    def send_gain(i, _):
        q = lax.rem(mine + i, QUADS)
        pltpu.make_async_remote_copy(
            src_ref=gb.at[:, pl.ds(pl.multiple_of(q * FEEDS, FEEDS), FEEDS)], dst_ref=gr.at[mine],
            send_sem=send_sem.at[0], recv_sem=recv_sem.at[0],
            device_id={"turn": q * GROUP + g}, device_id_type=MESH,
        ).start()
        return 0

    lax.fori_loop(1, QUADS, send_gain, 0)
    gr[mine] = gb[:, pl.ds(pl.multiple_of(mine * FEEDS, FEEDS), FEEDS)]

    history = [
        pltpu.make_async_remote_copy(
            src_ref=xv.at[:, pl.ds((slot + 1) * NFFT, NFFT)], dst_ref=xh.at[slot],
            send_sem=hist_sem.at[0, slot], recv_sem=hist_sem.at[1, slot],
            device_id={"tm": after}, device_id_type=MESH,
        )
        for slot in range(3)
    ]
    for slot in (2, 1, 0):
        history[slot].start()

    for i in (2, 3, 4):
        loads[i].wait()
    keep = jnp.where(tm > 0, 1.0, 0.0).astype(F32)

    def frame_of(at):
        if at < 0:
            return xh[at + 3].astype(F32) * keep
        return xv[:, pl.ds(at * NFFT, NFFT)].astype(F32)

    def channelize(f):
        total = wv[0:1, :] * frame_of(f - 3)
        for p in range(1, TAPS):
            total = total + wv[p : p + 1, :] * frame_of(f - 3 + p)
        total = total.astype(BF16).astype(F32)
        parts = eight_forward([total[:, n * SHORT : (n + 1) * SHORT] for n in range(8)])
        for k1 in range(8):
            re, im = parts[k1] if k1 < 5 else parts[8 - k1]
            c, s = tv[k1, 0:1, :], -tv[k1, 1:2, :]
            if im is None:
                zr, zi = re * c, re * s
            elif k1 < 5:
                zr, zi = re * c - im * s, re * s + im * c
            else:
                zr, zi = re * c + im * s, re * s - im * c
            rows = pl.ds(pl.multiple_of(lax.rem(k1 + g, 8) * 16, 16), 16)
            zs[f, rows, 0:SHORT] = zr.astype(BF16)
            zs[f, rows, SHORT : 2 * SHORT] = zi.astype(BF16)

    contract = (((1,), (1,)), ((), ()))

    def transform(f):
        channels = lax.dot_general(fv[...], zs[f], contract, preferred_element_type=F32)
        return channels.reshape(GROUP, 16, 128).astype(BF16)

    def exchange_channels(part, source, target):
        def send_channels(i, _):
            to = lax.rem(g + i, GROUP)
            pltpu.make_async_remote_copy(
                src_ref=source.at[to], dst_ref=target.at[g],
                send_sem=chan_sem.at[0, part], recv_sem=chan_sem.at[1, part],
                device_id={"turn": base + to}, device_id_type=MESH,
            ).start()
            return 0

        lax.fori_loop(1, GROUP, send_channels, 0)
        target[g] = source[g]

    channelize(3)
    al[...] = transform(3)
    exchange_channels(0, al, rl)

    for f in (2, 1, 0):
        history[f].wait_recv()
        channelize(f)
        ab[:, f] = transform(f)
    exchange_channels(1, ab, ra)

    pltpu.make_async_copy(gr.at[pl.ds(0, QUADS - 1)], gr.at[pl.ds(0, QUADS - 1)], recv_sem.at[0]).wait()
    for half in range(2):
        got = gr[:, :, half * 128 : (half + 1) * 128].astype(F32).reshape(QUADS, 2, 8, 128)
        for b in range(3):
            split = got.reshape(2 ** (2 - b), 2, 2**b, 2, 8, 128)
            flat = (-1, 8, 128)
            low, high = swap(split[:, 0].reshape(flat), split[:, 1].reshape(flat), 0, 1 << b)
            part = (2 ** (2 - b), 2**b, 2, 8, 128)
            got = jnp.stack([low.reshape(part), high.reshape(part)], axis=1).reshape(QUADS, 2, 8, 128)
        gt[half] = got

    loads[6].wait()
    loads[5].wait()
    turned_rows = [lax.rem(g + i, 16) * 8 for i in range(16)]
    for f in (3, 2, 1, 0):
        if f >= 2:
            arrived = rl if f == 3 else ra
            rest = arrived.at[pl.ds(0, GROUP - 1)]
            pltpu.make_async_copy(rest, rest, chan_sem.at[1, 3 - f]).wait()
        for half in range(2):
            items = [half * 8 + i for i in range(8)]
            items = [(rl[i] if f == 3 else ra[i, f]).astype(F32) for i in items]
            items = gather(items, 16)
            for k1 in range(8):
                re, im = items[k1][:8], items[k1][8:]
                gre, gim = gt[half, k1, 0], gt[half, k1, 1]
                rows = pl.ds(pl.multiple_of((f // 2) * 128 + turned_rows[(f % 2) * 8 + k1], 8), 8)
                xs[rows, half * 128 : (half + 1) * 128] = gre * re - gim * im
                xs[rows, FEEDS + half * 128 : FEEDS + (half + 1) * 128] = gre * im + gim * re
    xb[...] = xs[...].astype(BF16)

    row3 = lax.broadcasted_iota(jnp.int32, (16, 8, 128), 1)
    x_me, z_me = lax.div(me, 64), lax.rem(xz, 16)
    x_at, y_at = [x_me * 16, 16 - x_me * 16], [lax.rem(y + c, 4) for c in range(4)]
    for c in range(4):
        to_y = y_at[c]
        both = lax.dot_general(
            bv[pl.ds(pl.multiple_of(to_y * 128, 128), 128), :], xb[...], contract, preferred_element_type=F32
        )
        low, high = both[:, :128].reshape(16, 8, 128), both[:, 128:].reshape(16, 8, 128)
        even = jnp.where(row3 < 4, low, pltpu.roll(high, 4, 1))
        odd = jnp.where(row3 < 4, pltpu.roll(low, 4, 1), high)
        sb[to_y] = jnp.stack([even, odd], axis=1).reshape(32, 8, 128).astype(BF16)

    def send_beams(c, x_by, z_to):
        to_y = y_at[c]
        to = x_at[x_by] + z_to
        pltpu.make_async_remote_copy(
            src_ref=sb.at[to_y, to], dst_ref=sr.at[me],
            send_sem=send_sem.at[2], recv_sem=beam_sem.at[c],
            device_id={"turn": to * 4 + to_y}, device_id_type=MESH,
        ).start()

    def send_far(i, _):
        z_to = lax.rem(z_me + 8 + (1 - 2 * lax.rem(i, 2)) * lax.div(i + 1, 2), 16)
        for c in range(4):
            for x_by in range(2):
                send_beams(c, x_by, z_to)
        return 0

    lax.fori_loop(0, 15, send_far, 0)
    for c in range(4):
        for x_by in range(2):
            if c + x_by > 0:
                send_beams(c, x_by, z_me)
    sr[me] = sb[y, xz]

    loads[7].wait()
    row = lax.broadcasted_iota(jnp.int32, (8, 128), 0)

    def phases(at, _):
        for e in range(4):
            scale = jnp.where((row & 2) == 0, disp[e], disp[4 + e])
            c, s = jnp.cos(scale * sv[pl.ds(at, 1), :]), jnp.sin(scale * sv[pl.ds(at, 1), :])
            ct[at, 0, e] = 0.5 * c
            ct[at, 1, e] = 0.5 * s
        return 0

    lax.fori_loop(0, GROUP, phases, 0)

    def east_west(zl, from_y):
        at = zl * 4 + from_y
        ns = [[None] * 4, [None] * 4]
        for c in range(4):
            one = sr[c * GROUP + at].astype(F32)
            two = sr[64 + c * GROUP + at].astype(F32)
            ns[0][c], ns[1][c] = swap(one, two, 0, 1)
        (r0, r1, r2, r3), (i0, i1, i2, i3) = ns
        ra_, rb_, rc_, rd_ = r0 + r2, r0 - r2, r1 + r3, r1 - r3
        ia_, ib_, ic_, id_ = i0 + i2, i0 - i2, i1 + i3, i1 - i3
        beams = [(ra_ + rc_, ia_ + ic_), (rb_ + id_, ib_ - rd_), (ra_ - rc_, ia_ - ic_), (rb_ - id_, ib_ + rd_)]
        chirped = []
        for e in range(4):
            re, im = beams[e]
            c, s = ct[at, 0, e], ct[at, 1, e]
            chirped.append((re * c - im * s, re * s + im * c))
        for r in range(2):
            even = swap(chirped[0][r], chirped[2][r], 0, 4)
            odd = swap(chirped[1][r], chirped[3][r], 0, 4)
            for h in range(2):
                first, second = swap(even[h], odd[h], 0, 2)
                vs[r, h, at, :8] = first
                vs[r, h, at, 8:] = second
        return from_y

    for c in range(4):
        count = 32 if c else 31
        pltpu.make_async_copy(sr.at[pl.ds(0, count)], sr.at[pl.ds(0, count)], beam_sem.at[c]).wait()
        lax.fori_loop(0, 4, east_west, lax.rem(y + 4 - c, 4))

    for r in range(2):
        for h in range(2):
            items = gather([vs[r, h, i] for i in range(GROUP)], 8)
            for k in range(GROUP):
                ys[2 * h + k // 8, k % 8, :, r * 128 : (r + 1) * 128] = items[k].astype(BF16)

    def synthesise(f):
        z = jnp.dot(ys[f].reshape(128, 256), iv[...], preferred_element_type=F32).reshape(8, 16, 512)
        re, im = [], []
        for k1 in range(8):
            zr, zi = z[k1, :, :SHORT], z[k1, :, SHORT:]
            c, s = tv[k1, 0:1, :], tv[k1, 1:2, :]
            re.append(zr * c - zi * s)
            im.append(zr * s + zi * c if k1 % 4 else None)
        outs = eight_inverse(
            re[0], re[1] + re[7], re[2] + re[6], re[3] + re[5], re[4],
            im[1] - im[7], im[2] - im[6], im[3] - im[5],
        )
        for n in range(8):
            wf[f, :, n * SHORT : (n + 1) * SHORT] = outs[n]
            if f < 3:
                wb[f, :, n * SHORT : (n + 1) * SHORT] = outs[n].astype(BF16)

    future = [
        pltpu.make_async_remote_copy(
            src_ref=wb.at[f], dst_ref=wr.at[f], send_sem=fut_sem.at[0, f], recv_sem=fut_sem.at[1, f],
            device_id={"tm": before}, device_id_type=MESH,
        )
        for f in range(3)
    ]
    for f in range(3):
        synthesise(f)
        future[f].start()
    synthesise(3)

    last = jnp.where(tm < 3, 1.0, 0.0).astype(F32)

    def place(f, total):
        for b in range(8):
            ov[b, :, f * NFFT : (f + 1) * NFFT] = total[2 * b : 2 * b + 2]

    def store_frame(f):
        store = pltpu.make_async_copy(
            ov.at[:, :, pl.ds(f * NFFT, NFFT)], out.at[:, :, pl.ds(f * NFFT, NFFT)], out_sem.at[f]
        )
        store.start()
        return store

    for f in range(FRAMES):
        total = wv[3:4, :] * wf[f]
        for p in range(1, FRAMES - f):
            total = total + wv[3 - p : 4 - p, :] * wf[f + p]
        if f == 0:
            place(0, total)
        else:
            pv[f - 1] = total
    stores = [store_frame(0)]
    for f in range(1, FRAMES):
        future[f - 1].wait_recv()
        total = pv[f - 1]
        for p in range(FRAMES - f, TAPS):
            total = total + (wv[3 - p : 4 - p, :] * last) * wr[f + p - 4].astype(F32)
        place(f, total)
        stores.append(store_frame(f))

    for copy in history + future:
        copy.wait_send()
    pltpu.make_async_copy(gr.at[pl.ds(0, QUADS - 1)], gr.at[pl.ds(0, QUADS - 1)], send_sem.at[0]).wait()
    for part, target in ((0, rl), (1, ra)):
        rest = target.at[pl.ds(0, GROUP - 1)]
        pltpu.make_async_copy(rest, rest, chan_sem.at[0, part]).wait()
    pltpu.make_async_copy(sr.at[pl.ds(0, 127)], sr.at[pl.ds(0, 127)], send_sem.at[2]).wait()
    for store in stores:
        store.wait()


def body(voltages, gains, dispersion):
    anywhere = pl.BlockSpec(memory_space=pl.ANY)
    vmem = pltpu.VMEM
    return pl.pallas_call(
        kernel,
        out_shape=jax.ShapeDtypeStruct((8, 2, FRAMES * NFFT), F32),
        in_specs=[anywhere, anywhere, pl.BlockSpec(memory_space=pltpu.SMEM)] + [anywhere] * 6,
        out_specs=anywhere,
        scratch_shapes=[
            vmem((16, FRAMES * NFFT), BF16),
            vmem((3, 16, NFFT), BF16),
            vmem((2, 8, 2048), F32),
            vmem((TAPS, NFFT), F32),
            vmem((8, 2, SHORT), F32),
            vmem((256, 512), BF16),
            vmem((256, 512), BF16),
            vmem((512, 512), BF16),
            vmem((GROUP, 128), F32),
            vmem((16, 2048), BF16),
            vmem((QUADS, 16, FEEDS), BF16),
            vmem((2, 8, 2, 8, 128), F32),
            vmem((FRAMES, 128, 512), BF16),
            vmem((GROUP, 16, 128), BF16),
            vmem((GROUP, 16, 128), BF16),
            vmem((GROUP, 3, 16, 128), BF16),
            vmem((GROUP, 3, 16, 128), BF16),
            vmem((256, 512), F32),
            vmem((256, 512), BF16),
            vmem((4, 32, 8, 128), BF16),
            vmem((128, 8, 128), BF16),
            vmem((GROUP, 2, 4, 8, 128), F32),
            vmem((2, 2, GROUP, 16, 128), F32),
            vmem((FRAMES, 8, 16, 256), BF16),
            vmem((FRAMES, 16, NFFT), F32),
            vmem((3, 16, NFFT), BF16),
            vmem((3, 16, NFFT), BF16),
            vmem((3, 16, NFFT), F32),
            vmem((8, 2, FRAMES * NFFT), F32),
            pltpu.SemaphoreType.DMA((8,)),
            pltpu.SemaphoreType.DMA((FRAMES,)),
            pltpu.SemaphoreType.DMA((3,)),
            pltpu.SemaphoreType.DMA((1,)),
            pltpu.SemaphoreType.DMA((2, 3)),
            pltpu.SemaphoreType.DMA((2, 2)),
            pltpu.SemaphoreType.DMA((4,)),
            pltpu.SemaphoreType.DMA((2, 3)),
        ],
        compiler_params=pltpu.CompilerParams(
            collective_id=0, has_side_effects=True, vmem_limit_bytes=60 * 1024 * 1024
        ),
        cost_estimate=pl.CostEstimate(flops=500_000_000, bytes_accessed=3_000_000, transcendentals=0),
    )(
        voltages, gains.transpose(0, 2, 1), dispersion,
        window_rows(), twiddle_rows(), forward_table(), inverse_table(), beam_table(), spacing_rows(),
    )


def solution(mesh):
    placed = (P("turn", "tm"), P(None, None, "turn"), P("turn"))
    return jax.shard_map(
        body, mesh=mesh, in_specs=placed, out_specs=P("turn", None, "tm"), check_vma=False
    )
```
